256 devices in a mesh: gx: 128 (over z, x_lo, y, core), gz: 2 (over x_hi).
Axes of the slice: x: 4 (x_hi: 2, x_lo: 2; x = x_hi * 2 + x_lo), y: 4, z: 8, core: 2. Of those that a mesh axis runs over, the one named last changes fastest.
Arguments:
- queries: bfloat16 [65536, 1024], P(('gx', 'gz')), may hold values from -8 to 8
- key_rows: bfloat16 [65536, 1024], P(('gx', 'gz')), may hold values from -8 to 8
- value_rows: bfloat16 [65536, 1024], P(('gx', 'gz')), may hold values from -6 to 6
- grad_out: bfloat16 [65536, 1024], P(('gx', 'gz')), may hold values from -6 to 6
- pattern: int32 [512, 6, 2], P(('gx', 'gz')), may hold values from 0 to 1, as said below
Outputs:
- attended: bfloat16 [65536, 1024], P(('gx', 'gz'))
- grad_query: bfloat16 [65536, 1024], P(('gx', 'gz'))
- grad_key: bfloat16 [65536, 1024], P(('gx', 'gz'))
- grad_value: bfloat16 [65536, 1024], P(('gx', 'gz'))
The draws below stay inside these ranges and needn't reach their ends.
Inputs may be any that keep to these rules, and one draw needn't show every extreme that they name: pattern[g, r, kb].
All inputs are finite; a program needn't handle non-finite values.
Results may differ from the reference program's by a relative error of at most 0.028.
Values may be sent and summed in bfloat16 or wider, within the bound.
No kernel may reach another device: no remote copies, remote signals or barrier semaphores. Data moves between devices by JAX's collectives and lax.ppermute only.
A program may use at most 128 MiB of HBM per device.

```python
import jax
import jax.numpy as jnp
from jax import lax

H = 16
HD = 64
BT = 128
NSRC = 6
QB = 2
F = 1024
SLABS = 128
HALVES = 2
SPAN = 32
TOKENS = 65536
QBLOCKS = 512


def draw_queries(key, part):
    key = jax.random.fold_in(key, 3)
    return jnp.clip(jax.random.normal(key, (TOKENS, F), jnp.float32), -6.0, 6.0).astype(jnp.bfloat16)


def draw_key_rows(key, part):
    key = jax.random.fold_in(key, 5)
    return jnp.clip(jax.random.normal(key, (TOKENS, F), jnp.float32), -6.0, 6.0).astype(jnp.bfloat16)


def draw_pattern(key, part):
    key = jax.random.fold_in(key, 7)
    rolled = jax.random.randint(key, (QBLOCKS, NSRC, QB), 0, 2 * SLABS)
    slab = (jnp.arange(QBLOCKS) // (HALVES * QB))[:, None, None]
    source = jnp.arange(NSRC)[None, :, None]
    near = rolled < SLABS
    far = rolled < slab + 1
    return jnp.where(source >= 4, far, near).astype(jnp.int32)


def block_scale(stream_key, dims, cuts, least, top_value):
    factor_of = 1.0
    for axis_at, shards_of in cuts:
        steps = jax.random.uniform(jax.random.fold_in(jax.random.fold_in(stream_key, 6), axis_at), (shards_of,), jnp.float32, least / len(cuts), top_value / len(cuts))
        factor_of = factor_of * jnp.repeat(jnp.exp(steps), dims[axis_at] // shards_of).reshape((-1,) + (1,) * (len(dims) - 1 - axis_at))
    return factor_of


def centred(rng, shape, deviation, most, cuts=(), kind=jnp.bfloat16):
    result = deviation * jax.random.normal(rng, shape, jnp.float32)
    if cuts:
        result = result * block_scale(rng, shape, cuts, -0.22, 0.18)
    return jnp.clip(result, -most, most).astype(kind)


def setup_inputs(seed: int = 0) -> dict:
    seeds = jax.random.split(jax.random.key(seed), 6)
    queries = draw_queries(jax.random.fold_in(seeds[5], 71), 0)
    key_rows = draw_key_rows(jax.random.fold_in(seeds[5], 71), 0)
    value_rows = centred(seeds[2], (TOKENS, F), 1.0, 6.0, ((0, 256),))
    grad_out = centred(seeds[3], (TOKENS, F), 1.0, 6.0, ((0, 256),))
    pattern = draw_pattern(jax.random.fold_in(seeds[5], 71), 0)
    return dict(queries=queries, key_rows=key_rows, value_rows=value_rows, grad_out=grad_out, pattern=pattern)


def head_pass(query_head, grad_head, key_head, value_head, mask, scale):
    scores = jnp.dot(query_head, key_head.T, preferred_element_type=jnp.float32) * scale
    masked = jnp.where(mask, scores, -jnp.inf)
    peak = jnp.max(masked, axis=1, keepdims=True)
    expo = jnp.exp(masked - peak)
    probs = expo / jnp.sum(expo, axis=1, keepdims=True)
    probs_low = probs.astype(jnp.bfloat16)
    output = jnp.dot(probs_low, value_head, preferred_element_type=jnp.float32)
    out_low = output.astype(jnp.bfloat16)
    delta = jnp.sum(grad_head.astype(jnp.float32) * out_low.astype(jnp.float32), axis=1, keepdims=True)
    dprobs = jnp.dot(grad_head, value_head.T, preferred_element_type=jnp.float32)
    dscores_low = (probs * (dprobs - delta)).astype(jnp.bfloat16)
    grad_q = jnp.dot(dscores_low, key_head, preferred_element_type=jnp.float32) * scale
    grad_k = jnp.dot(dscores_low.T, query_head, preferred_element_type=jnp.float32) * scale
    grad_v = jnp.dot(probs_low.T, grad_head, preferred_element_type=jnp.float32)
    return out_low, grad_q, grad_k, grad_v


def device_pass(query_dev, grad_dev, keys_all, values_all, active):
    rows = query_dev.shape[0]
    own_block = (jnp.arange(NSRC)[None, :, None] == 0) & (jnp.arange(QB)[:, None, None] == jnp.arange(QB)[None, None, :])
    allowed = (active == 1) | own_block
    small = allowed.reshape(QB, NSRC * QB)
    mask = jnp.broadcast_to(small[:, None, :, None], (QB, BT, NSRC * QB, BT)).reshape(rows, NSRC * rows)
    scale = HD ** -0.5

    def split_heads(array):
        return array.reshape(array.shape[0], H, HD).transpose(1, 0, 2)

    def join_heads(array):
        return array.transpose(1, 0, 2).reshape(array.shape[1], H * HD)

    def one_head(operands):
        return head_pass(operands[0], operands[1], operands[2], operands[3], mask, scale)

    out_low, grad_q, grad_k, grad_v = lax.map(one_head, (split_heads(query_dev), split_heads(grad_dev), split_heads(keys_all), split_heads(values_all)))
    return join_heads(out_low), join_heads(grad_q).astype(jnp.bfloat16), join_heads(grad_k).astype(jnp.bfloat16), join_heads(grad_v).astype(jnp.bfloat16)


def reference(queries, key_rows, value_rows, grad_out, pattern):
    rows = QB * BT
    features = queries.shape[1]
    shape = (SLABS, HALVES, rows, features)
    query_grid = queries.reshape(shape)
    key_grid = key_rows.reshape(shape)
    value_grid = value_rows.reshape(shape)
    grad_grid = grad_out.reshape(shape)
    pattern_grid = pattern.reshape(SLABS, HALVES, QB, NSRC, QB)
    moves = ((0, 0), (0, 1), (-1, 0), (1, 0), (-SPAN, 0), (SPAN, 0))

    def step(carry, slab):
        key_acc, value_acc = carry
        outs = []
        grads = []
        for half in range(HALVES):
            places = [((slab + move) % SLABS, half ^ flip) for move, flip in moves]
            keys_all = jnp.concatenate([key_grid[place[0], place[1]] for place in places], axis=0)
            values_all = jnp.concatenate([value_grid[place[0], place[1]] for place in places], axis=0)
            out_low, grad_q, grad_k, grad_v = device_pass(query_grid[slab, half], grad_grid[slab, half], keys_all, values_all, pattern_grid[slab, half])
            for index, place in enumerate(places):
                key_acc = key_acc.at[place[0], place[1]].add(grad_k[index * rows:(index + 1) * rows].astype(jnp.float32))
                value_acc = value_acc.at[place[0], place[1]].add(grad_v[index * rows:(index + 1) * rows].astype(jnp.float32))
            outs.append(out_low)
            grads.append(grad_q)
        return (key_acc, value_acc), (jnp.stack(outs), jnp.stack(grads))

    zeros = jnp.zeros(shape, jnp.float32)
    (key_acc, value_acc), (outs, grads) = lax.scan(step, (zeros, zeros), jnp.arange(SLABS, dtype=jnp.int32))
    total = SLABS * HALVES * rows
    return (outs.reshape(total, features), grads.reshape(total, features),
            key_acc.astype(jnp.bfloat16).reshape(total, features), value_acc.astype(jnp.bfloat16).reshape(total, features))
```

```python
import jax
import jax.numpy as jnp
from jax import lax
from jax.experimental import pallas as pl
from jax.experimental.pallas import tpu as pltpu
from jax.sharding import PartitionSpec as P

HD = 64
BT = 128
NSRC = 6
QB = 2
ROWS = QB * BT
PAIR = 2 * HD
F = 1024
PAIRS = F // PAIR
SCALE = HD**-0.5

bf16 = jnp.bfloat16
f32 = jnp.float32


def nt(a, b):
    return lax.dot_general(a, b, (((1,), (1,)), ((), ())), preferred_element_type=f32)


def nn(a, b):
    return lax.dot_general(a, b, (((1,), (0,)), ((), ())), preferred_element_type=f32)


def pick(x, head):
    lanes = lax.broadcasted_iota(jnp.int32, x.shape, 1)
    mine = (lanes < HD) if head == 0 else (lanes >= HD)
    return jnp.where(mine, x, jnp.zeros_like(x))


def merge(x0, x1):
    lanes = lax.broadcasted_iota(jnp.int32, (ROWS, PAIR), 1)
    return jnp.where(lanes < HD, x0, x1)


def source_cols(r):
    return slice(r * ROWS, (r + 1) * ROWS)


def probs_kernel(pattern, q_ref, grad_ref, *refs):
    k_refs = refs[:NSRC]
    p_ref, scaled_ref, inv_ref = refs[NSRC : NSRC + 3]
    dv_refs = refs[NSRC + 3 : 2 * NSRC + 3]
    s_ref = refs[2 * NSRC + 3]
    q = q_ref[...] * bf16(SCALE)
    grad = grad_ref[...].astype(f32)
    invs = []
    scaled = []
    for head in range(2):
        qh = pick(q, head)
        for r in range(NSRC):
            s = nt(qh, k_refs[r][...])
            for g in range(QB):
                rows = slice(g * BT, (g + 1) * BT)
                for kb in range(QB):
                    part = s[rows, kb * BT : (kb + 1) * BT]
                    if r != 0 or g != kb:
                        part = part + jnp.where(pattern[g, r, kb] == 1, 0.0, -jnp.inf)
                    first = r * ROWS + kb * BT
                    s_ref[rows, first : first + BT] = part
        s = s_ref[...]
        peak = jnp.max(s, axis=1, keepdims=True)
        expo = jnp.exp(s - peak)
        inv = 1.0 / jnp.sum(expo, axis=1, keepdims=True)
        p_ref[head] = expo.astype(bf16)
        invs.append(inv)
        scaled.append(pick((grad * inv).astype(bf16), head))
    inv_ref[...] = merge(invs[0], invs[1])
    scaled_ref[...] = scaled[0] + scaled[1]
    left0, left1 = scaled[0].T, scaled[1].T
    for r in range(NSRC):
        cols = source_cols(r)
        t = nn(left0, p_ref[0, :, cols]) + nn(left1, p_ref[1, :, cols])
        dv_refs[r][...] = t.T.astype(bf16)


def grads_kernel(q_ref, grad_ref, scaled_ref, inv_ref, p_ref, *refs):
    k_refs = refs[:NSRC]
    v_refs = refs[NSRC : 2 * NSRC]
    o_ref, dq_ref = refs[2 * NSRC : 2 * NSRC + 2]
    dk_refs = refs[2 * NSRC + 2 : 3 * NSRC + 2]
    ds_ref = refs[3 * NSRC + 2]
    q = q_ref[...] * bf16(SCALE)
    inv = inv_ref[...]
    acc = [None, None]
    for head in range(2):
        for r in range(NSRC):
            t = nn(p_ref[head, :, source_cols(r)], v_refs[r][...])
            acc[head] = t if r == 0 else acc[head] + t
    low = (merge(acc[0], acc[1]) * inv).astype(bf16)
    o_ref[...] = low
    prod = grad_ref[...].astype(f32) * low.astype(f32) * inv
    dq = [None, None]
    for head in range(2):
        delta = jnp.sum(pick(prod, head), axis=1, keepdims=True)
        scaled = pick(scaled_ref[...], head)
        for r in range(NSRC):
            cols = source_cols(r)
            dp = nt(scaled, v_refs[r][...])
            ds = (p_ref[head, :, cols].astype(f32) * (dp - delta)).astype(bf16)
            ds_ref[head, :, cols] = ds
            t = nn(ds, k_refs[r][...])
            dq[head] = t if r == 0 else dq[head] + t
    dq_ref[...] = (merge(dq[0], dq[1]) * SCALE).astype(bf16)
    left0, left1 = pick(q, 0).T, pick(q, 1).T
    for r in range(NSRC):
        cols = source_cols(r)
        t = nn(left0, ds_ref[0, :, cols]) + nn(left1, ds_ref[1, :, cols])
        dk_refs[r][...] = t.T.astype(bf16)


pair_block = pl.BlockSpec((ROWS, PAIR), lambda h: (0, h))
probs_block = pl.BlockSpec((2, ROWS, NSRC * ROWS), lambda h: (h, 0, 0))
tall = jax.ShapeDtypeStruct((ROWS, F), bf16)
PAIR_FLOPS = 2 * 2 * ROWS * NSRC * ROWS * HD


def probs_pass(pattern, queries, grad_out, keys):
    outs = pl.pallas_call(
        probs_kernel,
        grid=(PAIRS,),
        in_specs=[pl.BlockSpec(memory_space=pltpu.SMEM)] + [pair_block] * (2 + NSRC),
        out_specs=[probs_block] + [pair_block] * (2 + NSRC),
        out_shape=[
            jax.ShapeDtypeStruct((2 * PAIRS, ROWS, NSRC * ROWS), bf16),
            tall,
            jax.ShapeDtypeStruct((ROWS, F), f32),
        ]
        + [tall] * NSRC,
        scratch_shapes=[pltpu.VMEM((ROWS, NSRC * ROWS), f32)],
        compiler_params=pltpu.CompilerParams(vmem_limit_bytes=40 * 2**20),
        cost_estimate=pl.CostEstimate(
            flops=16 * PAIRS * PAIR_FLOPS, bytes_accessed=24 * 2**20, transcendentals=0
        ),
        name="probs_pass",
    )(pattern, queries, grad_out, *keys)
    return outs[0], outs[1], outs[2], outs[3:]


def grads_pass(queries, grad_out, scaled, inv, probs, keys, values):
    outs = pl.pallas_call(
        grads_kernel,
        grid=(PAIRS,),
        in_specs=[pair_block] * 4 + [probs_block] + [pair_block] * (2 * NSRC),
        out_specs=[pair_block] * (2 + NSRC),
        out_shape=[tall] * (2 + NSRC),
        scratch_shapes=[pltpu.VMEM((2, ROWS, NSRC * ROWS), bf16)],
        compiler_params=pltpu.CompilerParams(vmem_limit_bytes=40 * 2**20),
        cost_estimate=pl.CostEstimate(
            flops=24 * PAIRS * PAIR_FLOPS, bytes_accessed=24 * 2**20, transcendentals=0
        ),
        name="grads_pass",
    )(queries, grad_out, scaled, inv, probs, *keys, *values)
    return outs[0], outs[1], outs[2:]


def from_partner(x):
    return lax.ppermute(x, "gz", [(0, 1), (1, 0)])


def shifted(x, by):
    peers = lax.axis_size("gx")
    return lax.ppermute(x, "gx", [(i, (i + by) % peers) for i in range(peers)])


def gather(x):
    reach = lax.axis_size("gx") // 4
    far_below, far_above = shifted(x, reach), shifted(x, -reach)
    below, above = shifted(x, 1), shifted(x, -1)
    return [x, from_partner(x), below, above, far_below, far_above]


def give_back(terms):
    reach = lax.axis_size("gx") // 4
    far_below, far_above = shifted(terms[4], -reach), shifted(terms[5], reach)
    below, above = shifted(terms[2], -1), shifted(terms[3], 1)
    partner = from_partner(terms[1])
    total = terms[0].astype(f32)
    for part in (partner, below, above, far_below, far_above):
        total = total + part.astype(f32)
    return total.astype(bf16)


def local(queries, key_rows, value_rows, grad_out, pattern):
    keys = gather(key_rows)
    values = gather(value_rows)
    probs, scaled, inv, value_terms = probs_pass(pattern, queries, grad_out, keys)
    grad_value = give_back(value_terms)
    attended, grad_query, key_terms = grads_pass(
        queries, grad_out, scaled, inv, probs, keys, values
    )
    grad_key = give_back(key_terms)
    return attended, grad_query, grad_key, grad_value


def solution(mesh):
    rows = P(("gx", "gz"), None)
    return jax.shard_map(
        local,
        mesh=mesh,
        in_specs=(rows, rows, rows, rows, P(("gx", "gz"), None, None)),
        out_specs=(rows,) * 4,
        check_vma=False,
    )
```

```python
import jax
import jax.numpy as jnp
from jax import lax
from jax.experimental import pallas as pl
from jax.experimental.pallas import tpu as pltpu
from jax.sharding import PartitionSpec as P

HD = 64
BT = 128
NSRC = 6
SOURCES = ['own', 'half', 'below', 'pair', 'chip', 'above']
OWN = SOURCES.index("own")
QB = 2
ROWS = QB * BT
PAIR = 2 * HD
F = 1024
PAIRS = F // PAIR
SCALE = HD**-0.5

bf16 = jnp.bfloat16
f32 = jnp.float32


def nt(a, b):
    return lax.dot_general(a, b, (((1,), (1,)), ((), ())), preferred_element_type=f32)


def nn(a, b):
    return lax.dot_general(a, b, (((1,), (0,)), ((), ())), preferred_element_type=f32)


def pick(x, head):
    lanes = lax.broadcasted_iota(jnp.int32, x.shape, 1)
    mine = (lanes < HD) if head == 0 else (lanes >= HD)
    return jnp.where(mine, x, jnp.zeros_like(x))


def merge(x0, x1):
    lanes = lax.broadcasted_iota(jnp.int32, (ROWS, PAIR), 1)
    return jnp.where(lanes < HD, x0, x1)


def pair_cols():
    return pl.ds(pl.multiple_of(pl.program_id(0) * PAIR, PAIR), PAIR)


def source_cols(r):
    return slice(r * ROWS, (r + 1) * ROWS)


def with_own(others, own):
    return [*others[:OWN], own, *others[OWN:]]


def probs_kernel(pattern, own_ref, *refs):
    q_ref, grad_ref = own_ref.at[0], own_ref.at[1]
    k_refs = with_own(refs[: NSRC - 1], own_ref.at[2])
    refs = refs[NSRC - 1 :]
    p_ref, scaled_ref, inv_ref = refs[:3]
    dv_refs = refs[3 : NSRC + 3]
    s_ref = refs[NSRC + 3]
    col = pair_cols()
    at = 2 * pl.program_id(0)
    q = q_ref[:, col]
    invs = []
    for head in range(2):
        qh = pick(q, head)
        for r in range(NSRC):
            s = nt(qh, k_refs[r][:, col])
            for g in range(QB):
                rows = slice(g * BT, (g + 1) * BT)
                for kb in range(QB):
                    part = s[rows, kb * BT : (kb + 1) * BT]
                    if r != OWN or g != kb:
                        part = part + jnp.where(pattern[g, r, kb] == 1, 0.0, -jnp.inf)
                    first = r * ROWS + kb * BT
                    s_ref[head, rows, first : first + BT] = part
        s = s_ref[head]
        peak = jnp.max(s, axis=1, keepdims=True)
        expo = jnp.exp(s - peak)
        invs.append(1.0 / jnp.sum(expo, axis=1, keepdims=True))
        p_ref[at + head] = expo.astype(bf16)
    inv = merge(invs[0], invs[1])
    inv_ref[:, col] = inv
    scaled = (grad_ref[:, col].astype(f32) * inv).astype(bf16)
    scaled_ref[:, col] = scaled
    left0, left1 = pick(scaled, 0).T, pick(scaled, 1).T
    for r in range(NSRC):
        cols = source_cols(r)
        t = nn(left0, p_ref[at, :, cols]) + nn(left1, p_ref[at + 1, :, cols])
        dv_refs[r][:, col] = t.T.astype(bf16)


def grads_kernel(own_ref, scaled_ref, inv_ref, p_ref, *refs):
    q_ref, grad_ref = own_ref.at[0], own_ref.at[1]
    k_refs = with_own(refs[: NSRC - 1], own_ref.at[2])
    v_refs = with_own(refs[NSRC - 1 : 2 * NSRC - 2], own_ref.at[3])
    refs = refs[2 * NSRC - 2 :]
    o_ref, dq_ref = refs[:2]
    dk_refs = refs[2 : NSRC + 2]
    ds_ref = refs[NSRC + 2]
    col = pair_cols()
    at = 2 * pl.program_id(0)

    def rows_of(weights, rights):
        sums = [None, None]
        for head in range(2):
            for r in range(NSRC):
                t = nn(weights(head, source_cols(r)), rights[r][:, col])
                sums[head] = t if r == 0 else sums[head] + t
        return merge(sums[0], sums[1])

    inv = inv_ref[:, col]
    low = (rows_of(lambda head, cols: p_ref[at + head, :, cols], v_refs) * inv).astype(bf16)
    o_ref[:, col] = low
    prod = grad_ref[:, col].astype(f32) * low.astype(f32) * inv
    scaled = scaled_ref[:, col]
    for head in range(2):
        delta = jnp.sum(pick(prod, head), axis=1, keepdims=True)
        left = pick(scaled, head)
        for r in range(NSRC):
            cols = source_cols(r)
            dp = nt(left, v_refs[r][:, col])
            p = p_ref[at + head, :, cols].astype(f32)
            ds_ref[head, :, cols] = (p * (dp - delta)).astype(bf16)
    dq = rows_of(lambda head, cols: ds_ref[head, :, cols], k_refs)
    dq_ref[:, col] = (dq * SCALE).astype(bf16)
    q = q_ref[:, col]
    left0, left1 = pick(q, 0).T, pick(q, 1).T
    for r in range(NSRC):
        cols = source_cols(r)
        t = nn(left0, ds_ref[0, :, cols]) + nn(left1, ds_ref[1, :, cols])
        dk_refs[r][:, col] = t.T.astype(bf16)


whole = pl.BlockSpec(memory_space=pltpu.VMEM)
tall = pltpu.VMEM((ROWS, F), bf16)
PAIR_FLOPS = 2 * 2 * ROWS * NSRC * ROWS * HD


def probs_pass(pattern, own, keys):
    outs = pl.pallas_call(
        probs_kernel,
        grid=(PAIRS,),
        in_specs=[pl.BlockSpec(memory_space=pltpu.SMEM)] + [whole] * NSRC,
        out_specs=[whole] * (3 + NSRC),
        out_shape=[
            pltpu.VMEM((2 * PAIRS, ROWS, NSRC * ROWS), bf16),
            tall,
            pltpu.VMEM((ROWS, F), f32),
        ]
        + [tall] * NSRC,
        scratch_shapes=[pltpu.VMEM((2, ROWS, NSRC * ROWS), f32)],
        compiler_params=pltpu.CompilerParams(vmem_limit_bytes=14 * 2**20),
        cost_estimate=pl.CostEstimate(
            flops=16 * PAIRS * PAIR_FLOPS, bytes_accessed=24 * 2**20, transcendentals=0
        ),
        name="probs_pass",
    )(pattern, own, *keys)
    return outs[0], outs[1], outs[2], outs[3:]


def grads_pass(own, scaled, inv, probs, keys, values):
    outs = pl.pallas_call(
        grads_kernel,
        grid=(PAIRS,),
        in_specs=[whole] * (2 + 2 * NSRC),
        out_specs=[whole] * (2 + NSRC),
        out_shape=[tall] * (2 + NSRC),
        scratch_shapes=[pltpu.VMEM((2, ROWS, NSRC * ROWS), bf16)],
        compiler_params=pltpu.CompilerParams(vmem_limit_bytes=14 * 2**20),
        cost_estimate=pl.CostEstimate(
            flops=24 * PAIRS * PAIR_FLOPS, bytes_accessed=24 * 2**20, transcendentals=0
        ),
        name="grads_pass",
    )(own, scaled, inv, probs, *keys, *values)
    return outs[0], outs[1], outs[2:]


def after(x, *done):
    return lax.optimization_barrier((x, *done))[0] if done else x


def move(x, way, sign):
    if way == "half":
        return lax.ppermute(x, "gz", [(0, 1), (1, 0)])
    peers = lax.axis_size("gx")
    if way in ("below", "above"):
        reach = (peers // 4) * (sign if way == "below" else -sign)
        return lax.ppermute(x, "gx", [(i, (i + reach) % peers) for i in range(peers)])
    first = 0 if way == "chip" else 1
    pairs = [(i, (i + 1) % peers) for i in range(first, peers, 2)]
    return lax.ppermute(x, "gx", pairs + [(b, a) for a, b in pairs])


def local(queries, key_rows, value_rows, grad_out, pattern):
    odd = lax.axis_index("gx") % 2
    at = dict(below=4, above=5, pair=2 + odd, half=1, chip=3 - odd, own=0)
    pattern = jnp.stack(
        [lax.dynamic_index_in_dim(pattern, at[n], 1, keepdims=False) for n in SOURCES], axis=1
    )
    k = {}
    for n in ['below', 'chip', 'pair', 'half', 'above']:
        k[n] = move(key_rows, n, 1)
    v = {}
    for n, deps in [['pair', []], ['half', ['half', 'pair', 'chip']], ['below', ['chip', 'pair']], ['chip', []], ['above', ['chip', 'pair']]]:
        v[n] = move(after(value_rows, *[k[d] for d in deps]), n, 1)
    keys = [k[n] for n in SOURCES if n != "own"]
    values = [v[n] for n in SOURCES if n != "own"]
    own = jnp.stack([queries * bf16(SCALE), grad_out, key_rows, value_rows])
    probs, scaled, inv, terms = probs_pass(pattern, own, keys)
    terms = dict(zip(SOURCES, terms))
    back = dict(own=terms["own"])
    for n, deps in [['below', ['pair', 'half', 'chip']], ['above', []], ['chip', []], ['pair', ['below']], ['half', []]]:
        back[n] = move(after(terms[n], *[v[d] for d in deps]), n, -1)
    total = back["own"].astype(f32)
    for n in ['half', 'chip', 'below', 'pair', 'above']:
        total = total + back[n].astype(f32)
    grad_value = total.astype(bf16)
    attended, grad_query, terms = grads_pass(own, scaled, inv, probs, keys, values)
    terms = dict(zip(SOURCES, terms))
    back2 = dict(own=terms["own"])
    for n, deps in [['below', ['half']], ['half', []], ['pair', ['below']], ['chip', ['below', 'above']], ['above', []]]:
        back2[n] = move(after(terms[n], *[back[d] for d in deps]), n, -1)
    total = back2["own"].astype(f32)
    for n in ['chip', 'above', 'below', 'pair', 'half']:
        total = total + back2[n].astype(f32)
    grad_key = total.astype(bf16)
    return attended, grad_query, grad_key, grad_value


def solution(mesh):
    rows = P(("gx", "gz"), None)
    return jax.shard_map(
        local,
        mesh=mesh,
        in_specs=(rows, rows, rows, rows, P(("gx", "gz"), None, None)),
        out_specs=(rows,) * 4,
        check_vma=False,
    )
```

```python
import jax
import jax.numpy as jnp
from jax import lax
from jax.experimental import pallas as pl
from jax.experimental.pallas import tpu as pltpu
from jax.sharding import PartitionSpec as P

HD = 64
BT = 128
NSRC = 6
SOURCES = ['above', 'pair', 'own', 'half', 'below', 'chip']
OWN = SOURCES.index("own")
QB = 2
ROWS = QB * BT
PAIR = 2 * HD
F = 1024
PAIRS = F // PAIR
SCALE = HD**-0.5

bf16 = jnp.bfloat16
f32 = jnp.float32


def nt(a, b):
    return lax.dot_general(a, b, (((1,), (1,)), ((), ())), preferred_element_type=f32)


def nn(a, b):
    return lax.dot_general(a, b, (((1,), (0,)), ((), ())), preferred_element_type=f32)


def pick(x, head):
    lanes = lax.broadcasted_iota(jnp.int32, x.shape, 1)
    mine = (lanes < HD) if head == 0 else (lanes >= HD)
    return jnp.where(mine, x, jnp.zeros_like(x))


def merge(x0, x1):
    lanes = lax.broadcasted_iota(jnp.int32, (ROWS, PAIR), 1)
    return jnp.where(lanes < HD, x0, x1)


def pair_cols():
    return pl.ds(pl.multiple_of(pl.program_id(0) * PAIR, PAIR), PAIR)


def source_cols(r):
    return slice(r * ROWS, (r + 1) * ROWS)


def with_own(others, own):
    return [*others[:OWN], own, *others[OWN:]]


def probs_kernel(pattern, own_ref, *refs):
    q_ref, grad_ref = own_ref.at[0], own_ref.at[1]
    k_refs = with_own(refs[: NSRC - 1], own_ref.at[2])
    refs = refs[NSRC - 1 :]
    p_ref, scaled_ref, inv_ref = refs[:3]
    dv_refs = refs[3 : NSRC + 3]
    s_ref = refs[NSRC + 3]
    col = pair_cols()
    at = 2 * pl.program_id(0)
    q = q_ref[:, col]
    invs = []
    for head in range(2):
        qh = pick(q, head)
        for r in range(NSRC):
            s = nt(qh, k_refs[r][:, col])
            for g in range(QB):
                rows = slice(g * BT, (g + 1) * BT)
                for kb in range(QB):
                    part = s[rows, kb * BT : (kb + 1) * BT]
                    if r != OWN or g != kb:
                        part = part + jnp.where(pattern[g, r, kb] == 1, 0.0, -jnp.inf)
                    first = r * ROWS + kb * BT
                    s_ref[head, rows, first : first + BT] = part
        s = s_ref[head]
        peak = jnp.max(s, axis=1, keepdims=True)
        expo = jnp.exp(s - peak)
        invs.append(1.0 / jnp.sum(expo, axis=1, keepdims=True))
        p_ref[at + head] = expo.astype(bf16)
    inv = merge(invs[0], invs[1])
    inv_ref[:, col] = inv
    scaled = (grad_ref[:, col].astype(f32) * inv).astype(bf16)
    scaled_ref[:, col] = scaled
    left0, left1 = pick(scaled, 0).T, pick(scaled, 1).T
    for r in range(NSRC):
        cols = source_cols(r)
        t = nn(left0, p_ref[at, :, cols]) + nn(left1, p_ref[at + 1, :, cols])
        dv_refs[r][:, col] = t.T.astype(bf16)


def grads_kernel(own_ref, scaled_ref, inv_ref, p_ref, *refs):
    q_ref, grad_ref = own_ref.at[0], own_ref.at[1]
    k_refs = with_own(refs[: NSRC - 1], own_ref.at[2])
    v_refs = with_own(refs[NSRC - 1 : 2 * NSRC - 2], own_ref.at[3])
    refs = refs[2 * NSRC - 2 :]
    o_ref, dq_ref = refs[:2]
    dk_refs = refs[2 : NSRC + 2]
    ds_ref = refs[NSRC + 2]
    col = pair_cols()
    at = 2 * pl.program_id(0)

    def rows_of(weights, rights):
        sums = [None, None]
        for head in range(2):
            for r in range(NSRC):
                t = nn(weights(head, source_cols(r)), rights[r][:, col])
                sums[head] = t if r == 0 else sums[head] + t
        return merge(sums[0], sums[1])

    inv = inv_ref[:, col]
    low = (rows_of(lambda head, cols: p_ref[at + head, :, cols], v_refs) * inv).astype(bf16)
    o_ref[:, col] = low
    prod = grad_ref[:, col].astype(f32) * low.astype(f32) * inv
    scaled = scaled_ref[:, col]
    for head in range(2):
        delta = jnp.sum(pick(prod, head), axis=1, keepdims=True)
        left = pick(scaled, head)
        for r in range(NSRC):
            cols = source_cols(r)
            dp = nt(left, v_refs[r][:, col])
            p = p_ref[at + head, :, cols].astype(f32)
            ds_ref[head, :, cols] = (p * (dp - delta)).astype(bf16)
    dq = rows_of(lambda head, cols: ds_ref[head, :, cols], k_refs)
    dq_ref[:, col] = (dq * SCALE).astype(bf16)
    q = q_ref[:, col]
    left0, left1 = pick(q, 0).T, pick(q, 1).T
    for r in range(NSRC):
        cols = source_cols(r)
        t = nn(left0, ds_ref[0, :, cols]) + nn(left1, ds_ref[1, :, cols])
        dk_refs[r][:, col] = t.T.astype(bf16)


whole = pl.BlockSpec(memory_space=pltpu.VMEM)
tall = pltpu.VMEM((ROWS, F), bf16)
PAIR_FLOPS = 2 * 2 * ROWS * NSRC * ROWS * HD


def probs_pass(pattern, own, keys):
    outs = pl.pallas_call(
        probs_kernel,
        grid=(PAIRS,),
        in_specs=[pl.BlockSpec(memory_space=pltpu.SMEM)] + [whole] * NSRC,
        out_specs=[whole] * (3 + NSRC),
        out_shape=[
            pltpu.VMEM((2 * PAIRS, ROWS, NSRC * ROWS), bf16),
            tall,
            pltpu.VMEM((ROWS, F), f32),
        ]
        + [tall] * NSRC,
        scratch_shapes=[pltpu.VMEM((2, ROWS, NSRC * ROWS), f32)],
        compiler_params=pltpu.CompilerParams(vmem_limit_bytes=14 * 2**20),
        cost_estimate=pl.CostEstimate(
            flops=16 * PAIRS * PAIR_FLOPS, bytes_accessed=24 * 2**20, transcendentals=0
        ),
        name="probs_pass",
    )(pattern, own, *keys)
    return outs[0], outs[1], outs[2], outs[3:]


def grads_pass(own, scaled, inv, probs, keys, values):
    outs = pl.pallas_call(
        grads_kernel,
        grid=(PAIRS,),
        in_specs=[whole] * (2 + 2 * NSRC),
        out_specs=[whole] * (2 + NSRC),
        out_shape=[tall] * (2 + NSRC),
        scratch_shapes=[pltpu.VMEM((2, ROWS, NSRC * ROWS), bf16)],
        compiler_params=pltpu.CompilerParams(vmem_limit_bytes=14 * 2**20),
        cost_estimate=pl.CostEstimate(
            flops=24 * PAIRS * PAIR_FLOPS, bytes_accessed=24 * 2**20, transcendentals=0
        ),
        name="grads_pass",
    )(own, scaled, inv, probs, *keys, *values)
    return outs[0], outs[1], outs[2:]


def after(x, *done):
    return lax.optimization_barrier((x, *done))[0] if done else x


def move(x, way, sign):
    if way == "half":
        return lax.ppermute(x, "gz", [(0, 1), (1, 0)])
    peers = lax.axis_size("gx")
    if way in ("below", "above"):
        reach = (peers // 4) * (sign if way == "below" else -sign)
        return lax.ppermute(x, "gx", [(i, (i + reach) % peers) for i in range(peers)])
    ends = [(i, (i + 1) % peers) for i in range(0 if way == "chip" else 1, peers, 2)]
    return lax.ppermute(x, "gx", ends + [(b, a) for a, b in ends])


def local(queries, key_rows, value_rows, grad_out, pattern):
    odd = lax.axis_index("gx") % 2
    at = dict(below=4, above=5, pair=2 + odd, half=1, chip=3 - odd, own=0)
    pattern = jnp.stack(
        [lax.dynamic_index_in_dim(pattern, at[n], 1, keepdims=False) for n in SOURCES], axis=1
    )
    own = jnp.stack([queries * bf16(SCALE), grad_out, key_rows, value_rows])
    k = {}
    for n in ['chip', 'below', 'half', 'above', 'pair']:
        k[n] = move(key_rows, n, 1)
    v = {}
    for n, deps in [['pair', []], ['half', ['half', 'pair', 'chip']], ['below', ['chip', 'pair']], ['chip', []], ['above', ['chip', 'pair']]]:
        x = after(value_rows, *[k[d] for d in deps])
        v[n] = move(x, n, 1)
    keys = [k[n] for n in SOURCES if n != "own"]
    values = [v[n] for n in SOURCES if n != "own"]
    probs, scaled, inv, terms = probs_pass(pattern, own, keys)
    terms = dict(zip(SOURCES, terms))
    back = dict(own=terms["own"])
    for n, deps in [['below', ['pair', 'half', 'chip']], ['above', []], ['chip', []], ['pair', ['below']], ['half', []]]:
        x = after(terms[n], *[v[d] for d in deps])
        back[n] = move(x, n, -1)
    total = back["own"].astype(f32)
    for n in ['half', 'chip', 'below', 'pair', 'above']:
        total = total + back[n].astype(f32)
    grad_value = total.astype(bf16)
    attended, grad_query, terms = grads_pass(own, scaled, inv, probs, keys, values)
    terms = dict(zip(SOURCES, terms))
    back2 = dict(own=terms["own"])
    for n, deps in [['below', ['half']], ['half', []], ['pair', ['below']], ['chip', ['below', 'above']], ['above', []]]:
        back2[n] = move(after(terms[n], *[back[d] for d in deps]), n, -1)
    total = back2["own"].astype(f32)
    for n in ['above', 'chip', 'pair', 'half', 'below']:
        total = total + back2[n].astype(f32)
    grad_key = total.astype(bf16)
    return attended, grad_query, grad_key, grad_value


def solution(mesh):
    rows = P(("gx", "gz"), None)
    return jax.shard_map(
        local,
        mesh=mesh,
        in_specs=(rows, rows, rows, rows, P(("gx", "gz"), None, None)),
        out_specs=(rows,) * 4,
        check_vma=False,
    )
```

```python
import jax
import jax.numpy as jnp
from jax import lax
from jax.experimental import pallas as pl
from jax.experimental.pallas import tpu as pltpu
from jax.sharding import PartitionSpec as P

HD = 64
BT = 128
NSRC = 6
SOURCES = ['above', 'pair', 'own', 'half', 'below', 'chip']
OWN = SOURCES.index("own")
QB = 2
ROWS = QB * BT
PAIR = 2 * HD
F = 1024
PAIRS = F // PAIR
SCALE = HD**-0.5

bf16 = jnp.bfloat16
f32 = jnp.float32


def nt(a, b):
    return lax.dot_general(a, b, (((1,), (1,)), ((), ())), preferred_element_type=f32)


def nn(a, b):
    return lax.dot_general(a, b, (((1,), (0,)), ((), ())), preferred_element_type=f32)


def pick(x, head):
    lanes = lax.broadcasted_iota(jnp.int32, x.shape, 1)
    mine = (lanes < HD) if head == 0 else (lanes >= HD)
    return jnp.where(mine, x, jnp.zeros_like(x))


def merge(x0, x1):
    lanes = lax.broadcasted_iota(jnp.int32, (ROWS, PAIR), 1)
    return jnp.where(lanes < HD, x0, x1)


def pair_cols():
    return pl.ds(pl.multiple_of(pl.program_id(0) * PAIR, PAIR), PAIR)


def source_cols(r):
    return slice(r * ROWS, (r + 1) * ROWS)


def with_own(others, own):
    return [*others[:OWN], own, *others[OWN:]]


def probs_kernel(pattern, own_ref, *refs):
    q_ref, grad_ref = own_ref.at[0], own_ref.at[1]
    k_refs = with_own(refs[: NSRC - 1], own_ref.at[2])
    refs = refs[NSRC - 1 :]
    p_ref, scaled_ref, inv_ref = refs[:3]
    dv_refs = refs[3 : NSRC + 3]
    s_ref = refs[NSRC + 3]
    col = pair_cols()
    at = 2 * pl.program_id(0)
    q = q_ref[:, col]
    invs = []
    for head in range(2):
        qh = pick(q, head)
        for r in range(NSRC):
            s = nt(qh, k_refs[r][:, col])
            for g in range(QB):
                rows = slice(g * BT, (g + 1) * BT)
                for kb in range(QB):
                    part = s[rows, kb * BT : (kb + 1) * BT]
                    if r != OWN or g != kb:
                        part = part + jnp.where(pattern[g, r, kb] == 1, 0.0, -jnp.inf)
                    first = r * ROWS + kb * BT
                    s_ref[head, rows, first : first + BT] = part
        s = s_ref[head]
        peak = jnp.max(s, axis=1, keepdims=True)
        expo = jnp.exp(s - peak)
        invs.append(1.0 / jnp.sum(expo, axis=1, keepdims=True))
        p_ref[at + head] = expo.astype(bf16)
    inv = merge(invs[0], invs[1])
    inv_ref[:, col] = inv
    scaled = (grad_ref[:, col].astype(f32) * inv).astype(bf16)
    scaled_ref[:, col] = scaled
    left0, left1 = pick(scaled, 0).T, pick(scaled, 1).T
    for r in range(NSRC):
        cols = source_cols(r)
        t = nn(left0, p_ref[at, :, cols]) + nn(left1, p_ref[at + 1, :, cols])
        dv_refs[r][:, col] = t.T.astype(bf16)


def grads_kernel(own_ref, scaled_ref, inv_ref, p_ref, *refs):
    q_ref, grad_ref = own_ref.at[0], own_ref.at[1]
    k_refs = with_own(refs[: NSRC - 1], own_ref.at[2])
    v_refs = with_own(refs[NSRC - 1 : 2 * NSRC - 2], own_ref.at[3])
    refs = refs[2 * NSRC - 2 :]
    o_ref, dq_ref = refs[:2]
    dk_refs = refs[2 : NSRC + 2]
    ds_ref = refs[NSRC + 2]
    col = pair_cols()
    at = 2 * pl.program_id(0)

    def rows_of(weights, rights):
        sums = [None, None]
        for head in range(2):
            for r in range(NSRC):
                t = nn(weights(head, source_cols(r)), rights[r][:, col])
                sums[head] = t if r == 0 else sums[head] + t
        return merge(sums[0], sums[1])

    inv = inv_ref[:, col]
    low = (rows_of(lambda head, cols: p_ref[at + head, :, cols], v_refs) * inv).astype(bf16)
    o_ref[:, col] = low
    prod = grad_ref[:, col].astype(f32) * low.astype(f32) * inv
    scaled = scaled_ref[:, col]
    for head in range(2):
        delta = jnp.sum(pick(prod, head), axis=1, keepdims=True)
        left = pick(scaled, head)
        for r in range(NSRC):
            cols = source_cols(r)
            dp = nt(left, v_refs[r][:, col])
            p = p_ref[at + head, :, cols].astype(f32)
            ds_ref[head, :, cols] = (p * (dp - delta)).astype(bf16)
    dq = rows_of(lambda head, cols: ds_ref[head, :, cols], k_refs)
    dq_ref[:, col] = (dq * SCALE).astype(bf16)
    q = q_ref[:, col]
    left0, left1 = pick(q, 0).T, pick(q, 1).T
    for r in range(NSRC):
        cols = source_cols(r)
        t = nn(left0, ds_ref[0, :, cols]) + nn(left1, ds_ref[1, :, cols])
        dk_refs[r][:, col] = t.T.astype(bf16)


whole = pl.BlockSpec(memory_space=pltpu.VMEM)
tall = pltpu.VMEM((ROWS, F), bf16)
PAIR_FLOPS = 2 * 2 * ROWS * NSRC * ROWS * HD


def probs_pass(pattern, own, keys):
    outs = pl.pallas_call(
        probs_kernel,
        grid=(PAIRS,),
        in_specs=[pl.BlockSpec(memory_space=pltpu.SMEM)] + [whole] * NSRC,
        out_specs=[whole] * (3 + NSRC),
        out_shape=[
            pltpu.VMEM((2 * PAIRS, ROWS, NSRC * ROWS), bf16),
            tall,
            pltpu.VMEM((ROWS, F), f32),
        ]
        + [tall] * NSRC,
        scratch_shapes=[pltpu.VMEM((2, ROWS, NSRC * ROWS), f32)],
        compiler_params=pltpu.CompilerParams(vmem_limit_bytes=14 * 2**20),
        cost_estimate=pl.CostEstimate(
            flops=16 * PAIRS * PAIR_FLOPS, bytes_accessed=24 * 2**20, transcendentals=0
        ),
        name="probs_pass",
    )(pattern, own, *keys)
    return outs[0], outs[1], outs[2], outs[3:]


def grads_pass(own, scaled, inv, probs, keys, values):
    outs = pl.pallas_call(
        grads_kernel,
        grid=(PAIRS,),
        in_specs=[whole] * (2 + 2 * NSRC),
        out_specs=[whole] * (2 + NSRC),
        out_shape=[tall] * (2 + NSRC),
        scratch_shapes=[pltpu.VMEM((2, ROWS, NSRC * ROWS), bf16)],
        compiler_params=pltpu.CompilerParams(vmem_limit_bytes=14 * 2**20),
        cost_estimate=pl.CostEstimate(
            flops=24 * PAIRS * PAIR_FLOPS, bytes_accessed=24 * 2**20, transcendentals=0
        ),
        name="grads_pass",
    )(own, scaled, inv, probs, *keys, *values)
    return outs[0], outs[1], outs[2:]


def after(x, *done):
    return lax.optimization_barrier((x, *done))[0] if done else x


def move(x, way, sign):
    if way == "half":
        return lax.ppermute(x, "gz", [(0, 1), (1, 0)])
    peers = lax.axis_size("gx")
    if way in ("below", "above"):
        reach = (peers // 4) * (sign if way == "below" else -sign)
        return lax.ppermute(x, "gx", [(i, (i + reach) % peers) for i in range(peers)])
    ends = [(i, (i + 1) % peers) for i in range(0 if way == "chip" else 1, peers, 2)]
    return lax.ppermute(x, "gx", ends + [(b, a) for a, b in ends])


def local(queries, key_rows, value_rows, grad_out, pattern):
    odd = lax.axis_index("gx") % 2
    at = dict(below=4, above=5, pair=2 + odd, half=1, chip=3 - odd, own=0)
    pattern = jnp.stack(
        [lax.dynamic_index_in_dim(pattern, at[n], 1, keepdims=False) for n in SOURCES], axis=1
    )
    own = jnp.stack([queries * bf16(SCALE), grad_out, key_rows, value_rows])
    k = {}
    for n in ['chip', 'below', 'half', 'above', 'pair']:
        k[n] = move(key_rows, n, 1)
    v = {}
    for n, deps in [['pair', []], ['half', ['half', 'pair', 'chip']], ['below', ['chip', 'pair']], ['chip', []], ['above', ['chip', 'pair']]]:
        x = after(value_rows, *[k[d] for d in deps])
        v[n] = move(x, n, 1)
    keys = [k[n] for n in SOURCES if n != "own"]
    values = [v[n] for n in SOURCES if n != "own"]
    probs, scaled, inv, terms = probs_pass(pattern, own, keys)
    terms = dict(zip(SOURCES, terms))
    back = dict(own=terms["own"])
    for n, deps in [['below', ['pair', 'half', 'chip']], ['above', []], ['chip', []], ['pair', ['below']], ['half', []]]:
        x = after(terms[n], *[v[d] for d in deps])
        back[n] = move(x, n, -1)
    total = back["own"].astype(f32)
    for n in ['half', 'chip', 'below', 'pair', 'above']:
        total = total + back[n].astype(f32)
    grad_value = total.astype(bf16)
    attended, grad_query, terms = grads_pass(own, scaled, inv, probs, keys, values)
    terms = dict(zip(SOURCES, terms))
    back2 = dict(own=terms["own"])
    for n, deps in [['below', ['half']], ['half', []], ['pair', []], ['chip', ['below', 'above']], ['above', []]]:
        back2[n] = move(after(terms[n], *[back[d] for d in deps]), n, -1)
    total = back2["own"].astype(f32)
    for n in ['above', 'chip', 'pair', 'half', 'below']:
        total = total + back2[n].astype(f32)
    grad_key = total.astype(bf16)
    return attended, grad_query, grad_key, grad_value


def solution(mesh):
    rows = P(("gx", "gz"), None)
    return jax.shard_map(
        local,
        mesh=mesh,
        in_specs=(rows, rows, rows, rows, P(("gx", "gz"), None, None)),
        out_specs=(rows,) * 4,
        check_vma=False,
    )
```
